32 devices in a mesh: rows: 8 (over z, y), snaps: 4 (over x, core).
Axes of the slice: x: 2, y: 2, z: 4, core: 2. Of those that a mesh axis runs over, the one named last changes fastest.
Arguments:
- stress: float32 [131072, 1024], P('rows', 'snaps'), may hold values from -80 to 80
- sketch: float32 [64, 1024], P(None, 'snaps'), may hold values from -0.1875 to 0.1875
Outputs:
- basis: float32 [64, 131072], P(None, ('rows', 'snaps'))
- coeffs: float32 [64, 1024], P(None, 'snaps')
- spectrum: float32 [64, 64], replicated
The draws below stay inside these ranges and needn't reach their ends.
All inputs are finite; a program needn't handle non-finite values.
Results may differ from the reference program's by a relative error of at most 0.0015.
Values sent between devices are 32-bit elements; how exact they have to be, the bound alone decides.
A program may use at most 128 MiB of HBM per device.

```python
import math
import jax
import jax.numpy as jnp
from jax import lax

K = 64
SNAPS = 1024
TOTAL_ROWS = 131072


def draw_stress(key, part):
    streams = jax.random.split(key, 4)
    mode_count = 2 * K
    fall_rate = math.log(12.0) / K
    strength_norm = math.sqrt(sum((math.exp(-2.0 * fall_rate * index) for index in range(mode_count))))
    mode_weights = jnp.exp(-fall_rate * jnp.arange(mode_count, dtype=jnp.float32)) / strength_norm
    noise_level = math.sqrt(SNAPS) / (25.0 * strength_norm)
    left_factor = jnp.clip(jax.random.normal(streams[0], (TOTAL_ROWS, mode_count), jnp.float32), -4.0, 4.0)
    right_factor = jnp.clip(jax.random.normal(streams[1], (mode_count, SNAPS), jnp.float32), -4.0, 4.0)
    background = jnp.clip(jax.random.normal(streams[2], (TOTAL_ROWS, SNAPS), jnp.float32), -4.0, 4.0)
    jitter = jnp.ones((TOTAL_ROWS, 1), jnp.float32)
    log_three = 1.0986123
    row_place = jnp.arange(TOTAL_ROWS, dtype=jnp.float32) / TOTAL_ROWS
    column_place = jnp.arange(SNAPS, dtype=jnp.float32) / SNAPS
    row_factor = jnp.exp(log_three * row_place)[:, None] * jitter
    column_factor = jnp.exp(log_three * column_place)[None, :]
    modal_part = jnp.dot(left_factor * mode_weights[None, :], right_factor, precision=lax.Precision.HIGHEST)
    values = (modal_part + noise_level * background) * row_factor * column_factor / 3.0
    return jnp.clip(values, -80.0, 80.0).astype(jnp.float32)


def block_scale(stream_key, shape, pieces, smallest, high):
    level = 1.0
    for position, parts in pieces:
        draws = jax.random.uniform(jax.random.fold_in(jax.random.fold_in(stream_key, 6), position), (parts,), jnp.float32, smallest / len(pieces), high / len(pieces))
        level = level * jnp.repeat(jnp.exp(draws), shape[position] // parts).reshape((-1,) + (1,) * (len(shape) - 1 - position))
    return level


def scatter_about(own_key, dims, width, limit, cuts=(), held_as=jnp.bfloat16):
    result = jax.random.normal(own_key, dims, jnp.float32) * width
    if len(cuts) > 0:
        result = block_scale(own_key, dims, cuts, -0.22, 0.18) * result
    return jnp.clip(result, min=-limit, max=limit).astype(held_as)


def setup_inputs(seed: int = 0) -> dict:
    splits = jax.random.split(jax.random.key(seed), 3)
    return {
        "stress": draw_stress(jax.random.fold_in(splits[2], 71), 0),
        "sketch": scatter_about(splits[1], (K, SNAPS), SNAPS ** -0.5, 0.1875, ((1, 4),), jnp.float32),
    }


def product(left_m, right_m, left_dim, right_dim):
    return lax.dot_general(left_m.astype(jnp.float32), right_m.astype(jnp.float32), (((left_dim,), (right_dim,)), ((), ())), precision=lax.Precision.HIGHEST, preferred_element_type=jnp.float32)

def inverse_factor(gram_total):
    lower = jnp.linalg.cholesky(gram_total)
    ident = jnp.eye(gram_total.shape[0], dtype=gram_total.dtype)
    return lax.linalg.triangular_solve(lower, ident, left_side=True, lower=True)

def orthonormal(panel):
    factor = inverse_factor(product(panel, panel, 1, 1))
    return product(factor, panel, 1, 0)

def reference(stress, sketch):
    operand = sketch
    basis = None
    for turn in range(2):
        panel = product(operand, stress, 1, 1)
        basis = orthonormal(panel)
        operand = product(basis, stress, 1, 0)
    scale = jnp.sqrt(jnp.float32(TOTAL_ROWS))
    spectrum = product(operand, operand, 1, 1) / SNAPS
    return (basis * scale, operand, spectrum)
```

```python
import functools
import math

import jax
import jax.numpy as jnp
from jax import lax
from jax.experimental import pallas as pl
from jax.experimental.pallas import tpu as pltpu
from jax.sharding import PartitionSpec as P

MESH = pl.DeviceIdType.MESH
F32 = jnp.float32
BF16 = jnp.bfloat16
CHUNK = 1024
HALF = CHUNK // 2
SLOTS = 4
PIECE = 128
TURNS = 2


def dot(left_m, right_m, left_dim, right_dim, precision=None):
    return lax.dot_general(
        left_m,
        right_m,
        (((left_dim,), (right_dim,)), ((), ())),
        precision=precision,
        preferred_element_type=F32,
    )


def dot_full(left_m, right_m, left_dim, right_dim):
    return dot(left_m, right_m, left_dim, right_dim, lax.Precision.HIGHEST)


def split(value):
    high = value.astype(BF16)
    low = (value - high.astype(F32)).astype(BF16)
    return high, low


def inverse_factor(gram):
    k = gram.shape[0]
    line = lax.broadcasted_iota(jnp.int32, (k, k), 0)
    lane = lax.broadcasted_iota(jnp.int32, (k, k), 1)
    wide_line = lax.broadcasted_iota(jnp.int32, (k, 2 * k), 0)
    ident = jnp.where(line == lane, 1.0, 0.0).astype(F32)
    table = jnp.concatenate([gram, ident], axis=1)
    for j in range(k - 1):
        row = table[j : j + 1, :]
        row = row / row[:, j : j + 1]
        column = jnp.where(wide_line > j, table[:, j : j + 1], 0.0)
        table = table - column * row
    diag = jnp.sum(jnp.where(line == lane, table[:, :k], 0.0), axis=1, keepdims=True)
    return table[:, k:] / jnp.sqrt(diag)


def kernel(
    ranks, scale, batch_total,
    stress, sketch, basis_out, coeffs_out, spectrum_out,
    stage, high, low, operand, part, got1, summed, got2, panel,
    acc, spread, landed, total, full, spect,
    stage_sem, send1, recv1, send2, recv2, send3, recv3,
    rs_send, rs_recv, ag_send, ag_recv, sp_send, sp_recv,
):
    groups = 4
    k = sketch.shape[0]
    width = stress.shape[1]
    chunks = part.shape[0]
    lines = k // ranks
    me_row = lax.axis_index("rows")
    me = lax.axis_index("snaps")
    mine = me % 2
    core = me + 1 - 2 * mine
    chip = (me + 2) % groups

    def load(c):
        slot = c % SLOTS
        return pltpu.make_async_copy(
            stress.at[pl.ds(c * CHUNK, CHUNK), :], stage.at[slot], stage_sem.at[slot]
        )

    for c in range(SLOTS):
        load(c).start()

    barrier = pltpu.get_barrier_semaphore()
    for d in range(1, ranks):
        pl.semaphore_signal(
            barrier, inc=1, device_id={"rows": (me_row + d) % ranks}, device_id_type=MESH
        )
    for d in range(1, groups):
        pl.semaphore_signal(
            barrier, inc=1, device_id={"snaps": (me + d) % groups}, device_id_type=MESH
        )

    def remote(src, dst, s_sem, r_sem, device):
        return pltpu.make_async_remote_copy(
            src_ref=src, dst_ref=dst, send_sem=s_sem, recv_sem=r_sem,
            device_id=device, device_id_type=MESH,
        )

    def hop1(t, c):
        return remote(
            part.at[c, 1 - mine], got1.at[t, c], send1.at[t, c], recv1.at[t, c], {"snaps": core}
        )

    def hop2(t, c):
        return remote(summed.at[c], got2.at[t, c], send2.at[t, c], recv2.at[t, c], {"snaps": chip})

    def hop3(t, c):
        return remote(
            panel.at[t, c, mine], panel.at[t, c, mine], send3.at[t, c], recv3.at[t, c],
            {"snaps": core},
        )

    def scatter(t, d):
        to = (me_row + d) % ranks
        return remote(
            spread.at[to], landed.at[t, d], rs_send.at[t, d], rs_recv.at[t, d], {"rows": to}
        )

    def gather(t, d):
        to = (me_row + d) % ranks
        return remote(
            total.at[t], full.at[t, me_row], ag_send.at[t, d], ag_recv.at[t, d], {"rows": to}
        )

    def share_spectrum(d):
        return remote(
            spect.at[0], spect.at[d], sp_send.at[d], sp_recv.at[d], {"snaps": (me + d) % groups}
        )

    def set_operand(value):
        h, l = split(value)
        operand[0:k, :] = h
        operand[k : 2 * k, :] = l

    def convert(c):
        slot = c % SLOTS
        load(c).wait()

        def body(p, carry):
            h, l = split(stage[slot, pl.ds(p * PIECE, PIECE), :])
            at = pl.ds(c * CHUNK + p * PIECE, PIECE)
            high[at, :] = h
            low[at, :] = l
            return carry

        lax.fori_loop(0, CHUNK // PIECE, body, 0)

        @pl.when(c + SLOTS < chunks)
        def _():
            load(c + SLOTS).start()

    def project(t, c):
        if t == 0:
            convert(c)
        for h in range(2):
            at = pl.ds(c * CHUNK + h * HALF, HALF)
            both = dot(operand[...], high[at, :], 1, 1)
            rest = dot(operand[0:k, :], low[at, :], 1, 1)
            part[c, h] = both[0:k] + (both[k : 2 * k] + rest)

    def add_cores(t, c):
        hop1(t, c).wait_recv()
        summed[c] = part[c, mine] + got1[t, c]
        hop2(t, c).start()

    def add_chips(t, c):
        hop2(t, c).wait_recv()
        panel[t, c, mine] = summed[c] + got2[t, c]
        hop3(t, c).start()

    def accumulate(t, c):
        hop3(t, c).wait_recv()
        for h in range(2):
            value = panel[t, c, h]
            hi, lo = split(value)
            at = pl.ds(c * CHUNK + h * HALF, HALF)
            both = dot(jnp.concatenate([hi, lo], axis=0), high[at, :], 1, 0)
            rest = dot(hi, low[at, :], 1, 0)
            acc[:, 0:width] += both[0:k] + (both[k : 2 * k] + rest)
            acc[:, width : width + k] += dot_full(value, value, 1, 1)

    set_operand(sketch[...])
    factor = None
    sums = None
    for t in range(TURNS):
        acc[...] = jnp.zeros_like(acc)
        project(t, 0)
        if t == 0:
            pl.semaphore_wait(barrier, ranks - 1 + groups - 1)
        hop1(t, 0).start()

        def first(c, carry, t=t):
            project(t, c)
            hop1(t, c).start()
            add_cores(t, c - 1)
            return carry

        lax.fori_loop(1, chunks, first, 0)
        add_cores(t, chunks - 1)
        add_chips(t, 0)

        def second(c, carry, t=t):
            add_chips(t, c)
            accumulate(t, c - 1)
            return carry

        lax.fori_loop(1, chunks, second, 0)
        accumulate(t, chunks - 1)

        for r in range(ranks):
            spread[r] = acc[r * lines : (r + 1) * lines, :]
        for d in range(1, ranks):
            scatter(t, d).start()
        value = spread[me_row]
        for d in range(1, ranks):
            scatter(t, d).wait_recv()
            value = value + landed[t, d]
        total[t] = value
        full[t, me_row] = value
        for d in range(1, ranks):
            gather(t, d).start()

        def drain(c, carry, t=t):
            hop1(t, c).wait_send()
            hop2(t, c).wait_send()
            hop3(t, c).wait_send()
            return carry

        lax.fori_loop(0, chunks, drain, 0)
        for d in range(1, ranks):
            scatter(t, d).wait_send()
            gather(t, d).wait_recv()
        for d in range(1, ranks):
            gather(t, d).wait_send()
        for r in range(ranks):
            acc[r * lines : (r + 1) * lines, :] = full[t, r]
        factor = inverse_factor(acc[:, width : width + k])
        sums = dot_full(factor, acc[:, 0:width], 1, 0)
        if t + 1 < TURNS:
            set_operand(sums)

    coeffs_out[...] = sums
    own = dot_full(sums, sums, 1, 1)
    spect[0] = own
    for d in range(1, groups):
        share_spectrum(d).start()
    per = chunks // groups
    scaled = factor * scale
    for i in range(per):
        for h in range(2):
            at = (i * 2 + h) * HALF
            basis_out[:, at : at + HALF] = dot_full(scaled, panel[TURNS - 1, me * per + i, h], 1, 0)
    value = None
    for d in range(1, groups):
        share_spectrum(d).wait()
    a = spect[0] + spect[2]
    b = spect[1] + spect[3]
    spectrum_out[...] = (a + b) / batch_total


def on_device(stress, sketch):
    rows_dev, width = stress.shape
    k = sketch.shape[0]
    groups = lax.axis_size("snaps")
    ranks = lax.axis_size("rows")
    share = rows_dev // groups
    chunks = rows_dev // CHUNK
    lines = k // ranks
    wide = width + 128
    scale = math.sqrt(float(rows_dev * ranks))
    vmem = pl.BlockSpec(memory_space=pltpu.VMEM)
    dma = pltpu.SemaphoreType.DMA
    return pl.pallas_call(
        functools.partial(kernel, ranks, scale, float(width * groups)),
        out_shape=(
            jax.ShapeDtypeStruct((k, share), F32),
            jax.ShapeDtypeStruct((k, width), F32),
            jax.ShapeDtypeStruct((k, k), F32),
        ),
        in_specs=[pl.BlockSpec(memory_space=pl.ANY), vmem],
        out_specs=(vmem, vmem, vmem),
        scratch_shapes=[
            pltpu.VMEM((SLOTS, CHUNK, width), F32),
            pltpu.VMEM((rows_dev, width), BF16),
            pltpu.VMEM((rows_dev, width), BF16),
            pltpu.VMEM((2 * k, width), BF16),
            pltpu.VMEM((chunks, 2, k, HALF), F32),
            pltpu.VMEM((TURNS, chunks, k, HALF), F32),
            pltpu.VMEM((chunks, k, HALF), F32),
            pltpu.VMEM((TURNS, chunks, k, HALF), F32),
            pltpu.VMEM((TURNS, chunks, 2, k, HALF), F32),
            pltpu.VMEM((k, wide), F32),
            pltpu.VMEM((ranks, lines, wide), F32),
            pltpu.VMEM((TURNS, ranks, lines, wide), F32),
            pltpu.VMEM((TURNS, lines, wide), F32),
            pltpu.VMEM((TURNS, ranks, lines, wide), F32),
            pltpu.VMEM((groups, k, k), F32),
            dma((SLOTS,)),
            dma((TURNS, chunks)),
            dma((TURNS, chunks)),
            dma((TURNS, chunks)),
            dma((TURNS, chunks)),
            dma((TURNS, chunks)),
            dma((TURNS, chunks)),
            dma((TURNS, ranks)),
            dma((TURNS, ranks)),
            dma((TURNS, ranks)),
            dma((TURNS, ranks)),
            dma((groups,)),
            dma((groups,)),
        ],
        compiler_params=pltpu.CompilerParams(
            collective_id=0, has_side_effects=True, vmem_limit_bytes=58 * 1024 * 1024
        ),
        cost_estimate=pl.CostEstimate(
            flops=24 * rows_dev * width * k, bytes_accessed=rows_dev * width * 4, transcendentals=0
        ),
    )(stress, sketch)


def solution(mesh):
    placed = (P("rows", "snaps"), P(None, "snaps"))
    return jax.shard_map(
        on_device,
        mesh=mesh,
        in_specs=placed,
        out_specs=(P(None, ("rows", "snaps")), P(None, "snaps"), P()),
        check_vma=False,
    )
```

```python
import functools
import math

import jax
import jax.numpy as jnp
from jax import lax
from jax.experimental import pallas as pl
from jax.experimental.pallas import tpu as pltpu
from jax.sharding import PartitionSpec as P

MESH = pl.DeviceIdType.MESH
F32 = jnp.float32
BF16 = jnp.bfloat16
CHUNK = 1024
HALF = CHUNK // 2
SLOTS = 4
PIECE = 128
TURNS = 2


def dot(left_m, right_m, left_dim, right_dim, precision=None):
    return lax.dot_general(
        left_m,
        right_m,
        (((left_dim,), (right_dim,)), ((), ())),
        precision=precision,
        preferred_element_type=F32,
    )


def dot_full(left_m, right_m, left_dim, right_dim):
    return dot(left_m, right_m, left_dim, right_dim, lax.Precision.HIGHEST)


def split(value):
    high = value.astype(BF16)
    low = (value - high.astype(F32)).astype(BF16)
    return high, low


def inverse_factor(gram):
    k = gram.shape[0]
    line = lax.broadcasted_iota(jnp.int32, (k, k), 0)
    lane = lax.broadcasted_iota(jnp.int32, (k, k), 1)
    wide_line = lax.broadcasted_iota(jnp.int32, (k, 2 * k), 0)
    ident = jnp.where(line == lane, 1.0, 0.0).astype(F32)
    table = jnp.concatenate([gram, ident], axis=1)
    for j in range(k - 1):
        row = table[j : j + 1, :]
        row = row / row[:, j : j + 1]
        column = jnp.where(wide_line > j, table[:, j : j + 1], 0.0)
        table = table - column * row
    diag = jnp.sum(jnp.where(line == lane, table[:, :k], 0.0), axis=1, keepdims=True)
    return table[:, k:] / jnp.sqrt(diag)


def kernel(
    ranks, batch_total,
    stress, sketch, share_out, factor_out, coeffs_out, spectrum_out,
    stage, high, low, operand, part, got1, summed, got2, panel,
    acc, spread, landed, total, full, spect, gram, grams, acc_gram, factor, whole,
    stage_sem, share_sem, send1, recv1, send2, recv2, send3, recv3,
    rs_send, rs_recv, ag_send, ag_recv, sp_send, sp_recv, gr_send, gr_recv,
):
    groups = 4
    k = sketch.shape[0]
    width = stress.shape[1]
    chunks = part.shape[0]
    lines = k // ranks
    me_row = lax.axis_index("rows")
    me = lax.axis_index("snaps")
    mine = me % 2
    core = me + 1 - 2 * mine
    chip = (me + 2) % groups

    def load(c):
        slot = c % SLOTS
        return pltpu.make_async_copy(
            stress.at[pl.ds(c * CHUNK, CHUNK), :], stage.at[slot], stage_sem.at[slot]
        )

    for c in range(SLOTS):
        load(c).start()

    barrier = pltpu.get_barrier_semaphore()
    for d in range(1, ranks):
        pl.semaphore_signal(
            barrier, inc=1, device_id={"rows": (me_row + d) % ranks}, device_id_type=MESH
        )
    for d in range(1, groups):
        pl.semaphore_signal(
            barrier, inc=1, device_id={"snaps": (me + d) % groups}, device_id_type=MESH
        )

    def remote(src, dst, s_sem, r_sem, device):
        return pltpu.make_async_remote_copy(
            src_ref=src, dst_ref=dst, send_sem=s_sem, recv_sem=r_sem,
            device_id=device, device_id_type=MESH,
        )

    def hop1(t, c):
        return remote(
            part.at[c, 1 - mine], got1.at[t, c], send1.at[t, c], recv1.at[t, c], {"snaps": core}
        )

    def hop2(t, c):
        return remote(summed.at[c], got2.at[t, c], send2.at[t, c], recv2.at[t, c], {"snaps": chip})

    def hop3(t, c):
        return remote(
            panel.at[t, c, mine], panel.at[t, c, mine], send3.at[t, c], recv3.at[t, c],
            {"snaps": core},
        )

    def scatter(t, d):
        to = (me_row + d) % ranks
        return remote(
            spread.at[to], landed.at[t, d], rs_send.at[t, d], rs_recv.at[t, d], {"rows": to}
        )

    def gather(t, d):
        to = (me_row + d) % ranks
        return remote(
            total.at[t], full.at[t, me_row], ag_send.at[t, d], ag_recv.at[t, d], {"rows": to}
        )

    def give_gram(d):
        return remote(
            gram, grams.at[me_row], gr_send.at[d], gr_recv.at[d], {"rows": (me_row + d) % ranks}
        )

    def share_spectrum(d):
        return remote(
            spect.at[0], spect.at[d], sp_send.at[d], sp_recv.at[d], {"snaps": (me + d) % groups}
        )

    def share_copy():
        per = chunks // groups
        return pltpu.make_async_copy(whole.at[pl.ds(me * per, per)], share_out, share_sem)

    def set_operand(value):
        h, l = split(value)
        operand[0:k, :] = h
        operand[k : 2 * k, :] = l

    def convert(c):
        slot = c % SLOTS
        load(c).wait()

        def body(p, carry):
            h, l = split(stage[slot, pl.ds(p * PIECE, PIECE), :])
            at = pl.ds(c * CHUNK + p * PIECE, PIECE)
            high[at, :] = h
            low[at, :] = l
            return carry

        lax.fori_loop(0, CHUNK // PIECE, body, 0)

        @pl.when(c + SLOTS < chunks)
        def _():
            load(c + SLOTS).start()

    def project(t, c):
        if t == 0:
            convert(c)
        for h in range(2):
            at = pl.ds(c * CHUNK + h * HALF, HALF)
            both = dot(operand[...], high[at, :], 1, 1)
            rest = dot(operand[0:k, :], low[at, :], 1, 1)
            part[c, h] = both[0:k] + (both[k : 2 * k] + rest)

    def add_cores(t, c):
        hop1(t, c).wait_recv()
        summed[c] = part[c, mine] + got1[t, c]
        hop2(t, c).start()

    def add_chips(t, c):
        hop2(t, c).wait_recv()
        panel[t, c, mine] = summed[c] + got2[t, c]
        hop3(t, c).start()

    def accumulate(t, c):
        hop3(t, c).wait_recv()
        for h in range(2):
            value = panel[t, c, h]
            if t > 0:
                value = dot_full(factor[...], value, 1, 0)
                whole[c, h] = value
            hi, lo = split(value)
            at = pl.ds(c * CHUNK + h * HALF, HALF)
            both = dot(jnp.concatenate([hi, lo], axis=0), high[at, :], 1, 0)
            rest = dot(hi, low[at, :], 1, 0)
            acc[:, 0:width] += both[0:k] + (both[k : 2 * k] + rest)
            acc[:, width : width + k] += dot_full(value, value, 1, 1)

    set_operand(sketch[...])
    for t in range(TURNS):
        acc[...] = jnp.zeros_like(acc)
        project(t, 0)
        if t == 0:
            pl.semaphore_wait(barrier, ranks - 1 + groups - 1)
        hop1(t, 0).start()

        def first(c, carry, t=t):
            project(t, c)
            hop1(t, c).start()
            add_cores(t, c - 1)
            return carry

        lax.fori_loop(1, chunks, first, 0)
        add_cores(t, chunks - 1)
        if t > 0:
            factor[...] = inverse_factor(acc_gram[...])
        add_chips(t, 0)

        def second(c, carry, t=t):
            add_chips(t, c)
            accumulate(t, c - 1)
            return carry

        lax.fori_loop(1, chunks, second, 0)
        accumulate(t, chunks - 1)

        last = t == TURNS - 1
        if last:
            own_gram = acc[:, width : width + k]
            gram[...] = own_gram
            grams[me_row] = own_gram
            for d in range(1, ranks):
                give_gram(d).start()
        for r in range(ranks):
            spread[r] = acc[r * lines : (r + 1) * lines, :]
        for d in range(1, ranks):
            scatter(t, d).start()
        if last:
            for d in range(1, ranks):
                give_gram(d).wait_recv()
            gram_total = grams[0]
            for r in range(1, ranks):
                gram_total = gram_total + grams[r]
        value = spread[me_row]
        for d in range(1, ranks):
            scatter(t, d).wait_recv()
            value = value + landed[t, d]
        total[t] = value
        full[t, me_row] = value
        for d in range(1, ranks):
            gather(t, d).start()
        if last:
            share_copy().start()
            final = inverse_factor(gram_total)

        def drain(c, carry, t=t):
            hop1(t, c).wait_send()
            hop2(t, c).wait_send()
            hop3(t, c).wait_send()
            return carry

        lax.fori_loop(0, chunks, drain, 0)
        for d in range(1, ranks):
            scatter(t, d).wait_send()
        for d in range(1, ranks):
            gather(t, d).wait_recv()
        for r in range(ranks):
            acc[r * lines : (r + 1) * lines, :] = full[t, r]
        if not last:
            set_operand(acc[:, 0:width])
            acc_gram[...] = acc[:, width : width + k]

    sums = dot_full(final, acc[:, 0:width], 1, 0)
    coeffs_out[...] = sums
    factor_out[...] = final
    spect[0] = dot_full(sums, sums, 1, 1)
    for d in range(1, groups):
        share_spectrum(d).start()

    for d in range(1, ranks):
        give_gram(d).wait_send()
        for t in range(TURNS):
            gather(t, d).wait_send()
    share_copy().wait()
    for d in range(1, groups):
        share_spectrum(d).wait()
    a = spect[0] + spect[2]
    b = spect[1] + spect[3]
    spectrum_out[...] = (a + b) / batch_total


def finish(scale, factor, share, coeffs, spectrum, basis_out, coeffs_out, spectrum_out):
    scaled = factor[...] * scale
    for h in range(2):
        basis_out[:, h * HALF : (h + 1) * HALF] = dot_full(scaled, share[0, h], 1, 0)
    coeffs_out[...] = coeffs[...]
    spectrum_out[...] = spectrum[...]


def on_device(stress, sketch):
    rows_dev, width = stress.shape
    k = sketch.shape[0]
    groups = lax.axis_size("snaps")
    ranks = lax.axis_size("rows")
    share = rows_dev // groups
    chunks = rows_dev // CHUNK
    lines = k // ranks
    wide = width + 128
    scale = math.sqrt(float(rows_dev * ranks))
    vmem = pl.BlockSpec(memory_space=pltpu.VMEM)
    dma = pltpu.SemaphoreType.DMA
    per = chunks // groups
    part_out, factor, coeffs, spectrum = pl.pallas_call(
        functools.partial(kernel, ranks, float(width * groups)),
        out_shape=(
            jax.ShapeDtypeStruct((per, 2, k, HALF), F32),
            jax.ShapeDtypeStruct((k, k), F32),
            jax.ShapeDtypeStruct((k, width), F32),
            jax.ShapeDtypeStruct((k, k), F32),
        ),
        in_specs=[pl.BlockSpec(memory_space=pl.ANY), vmem],
        out_specs=(pl.BlockSpec(memory_space=pl.ANY), vmem, vmem, vmem),
        scratch_shapes=[
            pltpu.VMEM((SLOTS, CHUNK, width), F32),
            pltpu.VMEM((rows_dev, width), BF16),
            pltpu.VMEM((rows_dev, width), BF16),
            pltpu.VMEM((2 * k, width), BF16),
            pltpu.VMEM((chunks, 2, k, HALF), F32),
            pltpu.VMEM((TURNS, chunks, k, HALF), F32),
            pltpu.VMEM((chunks, k, HALF), F32),
            pltpu.VMEM((TURNS, chunks, k, HALF), F32),
            pltpu.VMEM((TURNS, chunks, 2, k, HALF), F32),
            pltpu.VMEM((k, wide), F32),
            pltpu.VMEM((ranks, lines, wide), F32),
            pltpu.VMEM((TURNS, ranks, lines, wide), F32),
            pltpu.VMEM((TURNS, lines, wide), F32),
            pltpu.VMEM((TURNS, ranks, lines, wide), F32),
            pltpu.VMEM((groups, k, k), F32),
            pltpu.VMEM((k, k), F32),
            pltpu.VMEM((ranks, k, k), F32),
            pltpu.VMEM((k, k), F32),
            pltpu.VMEM((k, k), F32),
            pltpu.VMEM((chunks, 2, k, HALF), F32),
            dma((SLOTS,)),
            dma,
            dma((TURNS, chunks)),
            dma((TURNS, chunks)),
            dma((TURNS, chunks)),
            dma((TURNS, chunks)),
            dma((TURNS, chunks)),
            dma((TURNS, chunks)),
            dma((TURNS, ranks)),
            dma((TURNS, ranks)),
            dma((TURNS, ranks)),
            dma((TURNS, ranks)),
            dma((groups,)),
            dma((groups,)),
            dma((ranks,)),
            dma((ranks,)),
        ],
        compiler_params=pltpu.CompilerParams(
            collective_id=0, has_side_effects=True, vmem_limit_bytes=58 * 1024 * 1024
        ),
        cost_estimate=pl.CostEstimate(
            flops=24 * rows_dev * width * k, bytes_accessed=rows_dev * width * 4, transcendentals=0
        ),
    )(stress, sketch)
    same = lambda i: (0, 0)
    return pl.pallas_call(
        functools.partial(finish, scale),
        grid=(per,),
        out_shape=(
            jax.ShapeDtypeStruct((k, share), F32),
            jax.ShapeDtypeStruct((k, width), F32),
            jax.ShapeDtypeStruct((k, k), F32),
        ),
        in_specs=[
            pl.BlockSpec((k, k), same),
            pl.BlockSpec((1, 2, k, HALF), lambda i: (i, 0, 0, 0)),
            pl.BlockSpec((k, width), same),
            pl.BlockSpec((k, k), same),
        ],
        out_specs=(
            pl.BlockSpec((k, CHUNK), lambda i: (0, i)),
            pl.BlockSpec((k, width), same),
            pl.BlockSpec((k, k), same),
        ),
    )(factor, part_out, coeffs, spectrum)


def solution(mesh):
    placed = (P("rows", "snaps"), P(None, "snaps"))
    return jax.shard_map(
        on_device,
        mesh=mesh,
        in_specs=placed,
        out_specs=(P(None, ("rows", "snaps")), P(None, "snaps"), P()),
        check_vma=False,
    )
```
